512 devices in a mesh: loop: 32 (over z_hi, x, core), mp: 16 (over z_lo, y).
Axes of the slice: x: 4, y: 8, z: 8 (z_hi: 4, z_lo: 2; z = z_hi * 2 + z_lo), core: 2. Of those that a mesh axis runs over, the one named last changes fastest.
Arguments:
- img_emb: bfloat16 [65536, 1536], P(('loop', 'mp')), may hold values from -0.15625 to 0.15625
- txt_emb: bfloat16 [65536, 1536], P(('loop', 'mp')), may hold values from -0.15625 to 0.15625
- hidden: bfloat16 [65536, 6144], P('loop', 'mp'), may hold values from -6 to 6
- positives: int32 [65536], P(('loop', 'mp')), may hold values from 0 to 65535, as said below
Outputs:
- text_grad: bfloat16 [65536, 1536], P(('loop', 'mp'))
- weight_grad: float32 [6144, 1536], P(('mp', 'loop'))
The draws below stay inside these ranges and needn't reach their ends.
Inputs may be any that keep to these rules, and one draw needn't show every extreme that they name: `positives`: the positive of an image row in block (g, m) is a text row of block ((g - k) mod 32, m) for some k < 4.
All inputs are finite; a program needn't handle non-finite values.
Results may differ from the reference program's by a relative error of at most 0.0059.
Values may be sent and summed in bfloat16 or wider, within the bound.
No kernel may reach another device: no remote copies, remote signals or barrier semaphores. Data moves between devices by JAX's collectives and lax.ppermute only.
A program may use at most 64 MiB of HBM per device.

```python
import math
import jax
import jax.numpy as jnp
from jax import lax

D = 1536
DH = 6144
IMG_DEV = 128
STEPS = 4
GROUPS = 32
SPLITS = 16
BATCH = 65536


def draw_positives(key, part):
    key = jax.random.fold_in(key, 7)
    first_key, second_key = jax.random.split(key)
    row_ids = jnp.arange(BATCH, dtype=jnp.int32)
    block_id = row_ids // IMG_DEV
    group_id = block_id // SPLITS
    member = block_id % SPLITS
    offset = jax.random.randint(first_key, (BATCH,), 0, STEPS, dtype=jnp.int32)
    within = jax.random.randint(second_key, (BATCH,), 0, IMG_DEV, dtype=jnp.int32)
    owner = (group_id - offset) % GROUPS
    return ((owner * SPLITS + member) * IMG_DEV + within).astype(jnp.int32)


def levels(rng, dims, shards, least, high):
    def one(axis_at, parts):
        heights = jax.random.uniform(jax.random.fold_in(jax.random.fold_in(rng, 6), axis_at), (parts,), jnp.float32, least / len(shards), high / len(shards))
        return jnp.repeat(jnp.exp(heights), dims[axis_at] // parts).reshape((-1,) + (1,) * (len(dims) - axis_at - 1))

    gain = one(*shards[0])
    for cut in shards[1:]:
        gain = gain * one(*cut)
    return gain


def scatter_about(stream_key, shape, spread, reach, cuts=(), held_as=jnp.bfloat16):
    values = jax.random.normal(stream_key, shape, jnp.float32) * spread
    if len(cuts) > 0:
        values = levels(stream_key, shape, cuts, -0.22, 0.18) * values
    return jnp.clip(values, min=-reach, max=reach).astype(held_as)


def setup_inputs(seed: int = 0) -> dict:
    key_list = jax.random.split(jax.random.key(seed), 5)
    img_emb = scatter_about(key_list[0], (BATCH, D), (D ** -0.5), 0.15625, ((0, 512),))
    txt_emb = scatter_about(key_list[1], (BATCH, D), (D ** -0.5), 0.15625, ((0, 512),))
    hidden = scatter_about(key_list[2], (BATCH, DH), 1.0, 6.0, ((0, 32), (1, 16)))
    positives = draw_positives(jax.random.fold_in(key_list[4], 71), 0)
    return {"img_emb": img_emb, "txt_emb": txt_emb, "hidden": hidden, "positives": positives}


SCALE_T = 10.0
BIAS_T = -1.0
EPSILON = 1e-06

def normalize(values):
    widened = values.astype(jnp.float32)
    inverse = lax.rsqrt(lax.optimization_barrier(jnp.sum(widened * widened, axis=-1, keepdims=True)) + EPSILON)
    return (widened * inverse, inverse)

def backward_norm(unit_rows, inverse, upstream):
    return (upstream - unit_rows * lax.optimization_barrier(jnp.sum(unit_rows * upstream, axis=-1, keepdims=True))) * inverse

def reference(img_emb, txt_emb, hidden, positives):
    image_unit, image_inv = normalize(img_emb)
    text_unit, text_inv = normalize(txt_emb)
    image_low = lax.optimization_barrier(image_unit.astype(jnp.bfloat16)).astype(jnp.float32)
    text_low = lax.optimization_barrier(text_unit.astype(jnp.bfloat16)).astype(jnp.float32)
    image_blocks = image_low.reshape(GROUPS, SPLITS, IMG_DEV, D)
    text_blocks = text_low.reshape(GROUPS, SPLITS, IMG_DEV, D)
    pos_blocks = positives.reshape(GROUPS, SPLITS, IMG_DEV)
    group_ids = jnp.arange(GROUPS, dtype=jnp.int32)[:, None, None, None]
    split_ids = jnp.arange(SPLITS, dtype=jnp.int32)[None, :, None, None]
    col_ids = jnp.arange(IMG_DEV, dtype=jnp.int32)[None, None, None, :]
    image_total = jnp.zeros((GROUPS, SPLITS, IMG_DEV, D), jnp.float32)
    text_total = jnp.zeros((GROUPS, SPLITS, IMG_DEV, D), jnp.float32)
    for offset in range(STEPS):
        moved = jnp.roll(text_blocks, offset, axis=0)
        scores = SCALE_T * jnp.einsum('gsrd,gsqd->gsrq', image_blocks, moved, precision=lax.Precision.HIGHEST) + BIAS_T
        owner = (group_ids - offset) % GROUPS
        columns = (owner * SPLITS + split_ids) * IMG_DEV + col_ids
        target = (pos_blocks[..., None] == columns).astype(jnp.float32)
        coefficient = (jax.nn.sigmoid(scores) - target).astype(jnp.bfloat16)
        coefficient = lax.optimization_barrier(coefficient).astype(jnp.float32)
        image_total = image_total + SCALE_T * jnp.einsum('gsrq,gsqd->gsrd', coefficient, moved, precision=lax.Precision.HIGHEST)
        text_part = SCALE_T * jnp.einsum('gsrq,gsrd->gsqd', coefficient, image_blocks, precision=lax.Precision.HIGHEST)
        text_total = text_total + jnp.roll(text_part, -offset, axis=0)
    image_grad = backward_norm(image_unit, image_inv, image_total.reshape(BATCH, D)).astype(jnp.bfloat16)
    text_grad = backward_norm(text_unit, text_inv, text_total.reshape(BATCH, D)).astype(jnp.bfloat16)
    weight_grad = jnp.dot(hidden.T, image_grad, preferred_element_type=jnp.float32) / math.sqrt(BATCH)
    return (text_grad, weight_grad)
```

```python
import math

import jax
import jax.numpy as jnp
from jax import lax
from jax.sharding import PartitionSpec as P

SCALE_T = 10.0
BIAS_T = -1.0
EPSILON = 1e-06

Z_HI, X, CORE, Z_LO, Y = 4, 4, 2, 2, 8


def moved(value, where):
    pairs = []
    for source in range(Z_HI * X * CORE * Z_LO * Y):
        rest, y = divmod(source, Y)
        rest, z_lo = divmod(rest, Z_LO)
        rest, core = divmod(rest, CORE)
        z_hi, x = divmod(rest, X)
        a, b, c, d, e = where(z_hi, x, core, z_lo, y)
        pairs.append((source, ((((a % Z_HI) * X + b % X) * CORE + c % CORE) * Z_LO + d % Z_LO) * Y + e % Y))
    return lax.ppermute(value, ("loop", "mp"), pairs)


def next_chip(by):
    def where(z_hi, x, core, z_lo, y):
        chip = z_hi * X + x + by
        return chip // X, chip % X, core, z_lo, y

    return where


def cross(sign):
    def where(z_hi, x, core, z_lo, y):
        chip = z_hi * X + x
        if sign > 0:
            chip += 2 * core
        else:
            chip -= 2 * (1 - core)
        return chip // X, chip % X, 1 - core, z_lo, y

    return where


def other_core(z_hi, x, core, z_lo, y):
    return z_hi, x, 1 - core, z_lo, y


def other_z_lo(z_hi, x, core, z_lo, y):
    return z_hi, x, core, 1 - z_lo, y


def normalize(values):
    widened = values.astype(jnp.float32)
    inverse = lax.rsqrt(jnp.sum(widened * widened, axis=1, keepdims=True) + EPSILON)
    return (widened * inverse, inverse)


def backward_norm(unit_rows, inverse, upstream):
    return (upstream - unit_rows * jnp.sum(unit_rows * upstream, axis=1, keepdims=True)) * inverse


def pair_terms(image_low, text_low, positives, first_col):
    scores = (
        SCALE_T
        * lax.dot_general(
            image_low, text_low, (((1,), (1,)), ((), ())), preferred_element_type=jnp.float32
        )
        + BIAS_T
    )
    columns = first_col + lax.broadcasted_iota(jnp.int32, scores.shape, 1)
    target = (positives[:, None] == columns).astype(jnp.float32)
    coefficient = (jax.nn.sigmoid(scores) - target).astype(jnp.bfloat16)
    image_part = SCALE_T * jnp.dot(coefficient, text_low, preferred_element_type=jnp.float32)
    text_part = SCALE_T * lax.dot_general(
        coefficient, image_low, (((0,), (0,)), ((), ())), preferred_element_type=jnp.float32
    )
    return (image_part, text_part)


def local(img_emb, txt_emb, hidden, positives):
    bf16 = jnp.bfloat16
    loop_index = lax.axis_index("loop")
    model_index = lax.axis_index("mp")
    core = loop_index % CORE
    x = (loop_index // CORE) % X
    z_hi = loop_index // (CORE * X)
    z_lo = model_index // Y
    groups = lax.axis_size("loop")
    splits = lax.axis_size("mp")
    rows, width = img_emb.shape
    half = width // Z_LO
    units = hidden.shape[1]
    share = units // groups

    text_unit, text_inv = normalize(txt_emb)
    text_low = text_unit.astype(bf16)
    two_back = moved(text_low, next_chip(1))
    crossed = moved(text_low, cross(1))
    swapped = moved(two_back, other_core)
    image_unit, image_inv = normalize(img_emb)
    image_low = image_unit.astype(bf16)

    hidden_other = moved(hidden, other_z_lo)
    place = lax.broadcasted_iota(jnp.int32, (units, Z_LO * units), 1)
    block = CORE * X * Z_HI
    at_core = (place // (Z_LO * units // CORE) + core) % CORE
    at_x = (place // (Z_LO * units // (CORE * X)) + x) % X
    at_z = (place // (Z_LO * share) + z_hi) % Z_HI
    unit = ((at_z * X + at_x) * CORE + at_core) * share + place % share
    here = lax.broadcasted_iota(jnp.int32, place.shape, 0) == unit
    which = (place // share) % Z_LO
    hidden_both = jnp.dot(
        hidden, (here & (which == 0)).astype(bf16), preferred_element_type=bf16
    ) + jnp.dot(hidden_other, (here & (which == 1)).astype(bf16), preferred_element_type=bf16)
    hidden_both = hidden_both.reshape(Z_LO, Y, rows, Z_LO * units).transpose(1, 0, 2, 3)
    hidden_both = hidden_both.reshape(Z_LO * Y * rows, Z_LO * units)

    image_total = jnp.zeros(img_emb.shape, jnp.float32)
    text_parts = []
    far = jnp.where(core == 0, 3, 1)
    for text_block, offset in ((text_low, 0), (two_back, 2), (crossed, far), (swapped, 4 - far)):
        owner = (loop_index - offset) % groups
        first_col = (owner * splits + model_index) * rows
        image_part, text_part = pair_terms(image_low, text_block, positives, first_col)
        image_total = image_total + image_part
        text_parts.append(text_part)
    image_grad = backward_norm(image_unit, image_inv, image_total).astype(bf16)

    left, right = image_grad[:, :half], image_grad[:, half:]
    first = z_lo == 0
    mine = jnp.where(first, left, right)
    theirs = moved(jnp.where(first, right, left), other_z_lo)
    both = jnp.where(first, jnp.stack([mine, theirs]), jnp.stack([theirs, mine]))
    gathered = lax.all_gather(
        both.reshape(Z_LO * rows, half),
        "mp",
        axis=0,
        tiled=True,
        axis_index_groups=[list(range(Y)), list(range(Y, Z_LO * Y))],
    )

    back = moved(text_parts[3].astype(bf16), other_core)
    back_two = moved((text_parts[1] + back.astype(jnp.float32)).astype(bf16), next_chip(-1))
    back_cross = moved(text_parts[2].astype(bf16), cross(-1))
    text_total = text_parts[0] + back_two.astype(jnp.float32) + back_cross.astype(jnp.float32)
    text_grad = backward_norm(text_unit, text_inv, text_total).astype(bf16)

    total = lax.dot_general(
        hidden_both, gathered, (((0,), (0,)), ((), ())), preferred_element_type=jnp.float32
    )
    part = total.shape[0] // CORE
    total = total[:part] + moved(total[part:].astype(bf16), other_core).astype(jnp.float32)
    part = part // X
    pieces = [
        moved(
            total[part * k : part * (k + 1)].astype(bf16),
            lambda z_hi, x, core, z_lo, y, k=k: (z_hi, x + k, core, z_lo, y),
        )
        for k in range(1, X)
    ]
    total = total[:part] + sum(piece.astype(jnp.float32) for piece in pieces)
    part = part // Z_HI
    pieces = [
        moved(
            total[part * k : part * (k + 1)].astype(bf16),
            lambda z_hi, x, core, z_lo, y, k=k: (z_hi + k, x, core, z_lo, y),
        )
        for k in range(1, Z_HI)
    ]
    total = total[:part] + sum(piece.astype(jnp.float32) for piece in pieces)
    total = total / math.sqrt(rows * splits * groups)
    own = total[:share]
    rest = moved(total[share:], other_z_lo)
    weight_share = jnp.where(
        first, jnp.concatenate([own, rest], axis=1), jnp.concatenate([rest, own], axis=1)
    )
    return (text_grad, weight_share)


def solution(mesh):
    in_specs = (
        P(("loop", "mp"), None),
        P(("loop", "mp"), None),
        P("loop", "mp"),
        P(("loop", "mp")),
    )
    out_specs = (P(("loop", "mp"), None), P(("mp", "loop"), None))
    return jax.shard_map(local, mesh=mesh, in_specs=in_specs, out_specs=out_specs, check_vma=False)
```

```python
import math

import jax
import jax.numpy as jnp
from jax import lax
from jax.sharding import PartitionSpec as P

SCALE_T = 10.0
BIAS_T = -1.0
EPSILON = 1e-06

Z_HI, X, CORE, Z_LO, Y = 4, 4, 2, 2, 8


def moved(value, where):
    pairs = []
    for source in range(Z_HI * X * CORE * Z_LO * Y):
        rest, y = divmod(source, Y)
        rest, z_lo = divmod(rest, Z_LO)
        rest, core = divmod(rest, CORE)
        z_hi, x = divmod(rest, X)
        target = where(z_hi, x, core, z_lo, y)
        if target is None:
            continue
        a, b, c, d, e = target
        pairs.append((source, ((((a % Z_HI) * X + b % X) * CORE + c % CORE) * Z_LO + d % Z_LO) * Y + e % Y))
    return lax.ppermute(value, ("loop", "mp"), pairs)


def next_chip(by):
    def where(z_hi, x, core, z_lo, y):
        chip = z_hi * X + x + by
        return chip // X, chip % X, core, z_lo, y

    return where


def cross(sign):
    def where(z_hi, x, core, z_lo, y):
        chip = z_hi * X + x
        if sign > 0 and core == 1 and x == X - 1:
            return None
        if sign > 0:
            chip += 2 * core
        else:
            chip -= 2 * (1 - core)
        return chip // X, chip % X, 1 - core, z_lo, y

    return where


def third_hop(z_hi, x, core, z_lo, y):
    return (z_hi, 1, 0, z_lo, y) if x == 0 and core == 1 else None


def zero_of(*values):
    return sum(jnp.minimum(jnp.abs(v[(0,) * v.ndim].astype(jnp.float32)), 0.0) for v in values)


def other_core(z_hi, x, core, z_lo, y):
    return z_hi, x, 1 - core, z_lo, y


def other_z_lo(z_hi, x, core, z_lo, y):
    return z_hi, x, core, 1 - z_lo, y


def normalize(values):
    widened = values.astype(jnp.float32)
    inverse = lax.rsqrt(jnp.sum(widened * widened, axis=1, keepdims=True) + EPSILON)
    return (widened * inverse, inverse)


def backward_norm(unit_rows, inverse, upstream):
    return (upstream - unit_rows * jnp.sum(unit_rows * upstream, axis=1, keepdims=True)) * inverse


def pair_terms(image_low, text_low, positives, first_col):
    scores = (
        SCALE_T
        * lax.dot_general(
            image_low, text_low, (((1,), (1,)), ((), ())), preferred_element_type=jnp.float32
        )
        + BIAS_T
    )
    columns = first_col + lax.broadcasted_iota(jnp.int32, scores.shape, 1)
    target = (positives[:, None] == columns).astype(jnp.float32)
    coefficient = (jax.nn.sigmoid(scores) - target).astype(jnp.bfloat16)
    image_part = SCALE_T * jnp.dot(coefficient, text_low, preferred_element_type=jnp.float32)
    return (image_part, coefficient)


def text_terms(image_low, coefficient, scale):
    return scale * lax.dot_general(
        coefficient, image_low, (((0,), (0,)), ((), ())), preferred_element_type=jnp.float32
    )


def local(img_emb, txt_emb, hidden, positives):
    bf16 = jnp.bfloat16
    loop_index = lax.axis_index("loop")
    model_index = lax.axis_index("mp")
    core = loop_index % CORE
    x = (loop_index // CORE) % X
    z_hi = loop_index // (CORE * X)
    z_lo = model_index // Y
    groups = lax.axis_size("loop")
    splits = lax.axis_size("mp")
    rows, width = img_emb.shape
    half = width // Z_LO
    units = hidden.shape[1]
    share = units // groups

    text_unit, text_inv = normalize(txt_emb)
    text_low = text_unit.astype(bf16)
    two_back = moved(text_low, next_chip(1))
    crossed = moved(text_low, cross(1))
    swapped = moved(two_back, other_core)
    crossed = jnp.where((x == 1) & (core == 0), moved(two_back, third_hop), crossed)
    image_unit, image_inv = normalize(img_emb)
    image_low = image_unit.astype(bf16)

    place = lax.broadcasted_iota(jnp.int32, (units, Z_LO * units), 1)
    block = CORE * X * Z_HI
    at_core = (place // (Z_LO * units // CORE) + core) % CORE
    at_x = (place // (Z_LO * units // (CORE * X)) + x) % X
    at_z = (place // (Z_LO * share) + z_hi) % Z_HI
    unit = ((at_z * X + at_x) * CORE + at_core) * share + place % share
    here = lax.broadcasted_iota(jnp.int32, place.shape, 0) == unit
    which = (place // share) % Z_LO
    pick = (here & (which == 0)).astype(bf16), (here & (which == 1)).astype(bf16)

    def both_units(own):
        other = moved(own, other_z_lo)
        mixed = jnp.dot(own, pick[0], preferred_element_type=bf16) + jnp.dot(
            other, pick[1], preferred_element_type=bf16
        )
        return other, mixed.reshape(Y, rows, Z_LO * units)

    early, low = both_units(hidden[: Y * rows])
    _, high = both_units(hidden[Y * rows :])
    hidden_both = jnp.stack([low, high], axis=1).reshape(Z_LO * Y * rows, Z_LO * units)

    image_total = jnp.zeros(img_emb.shape, jnp.float32)
    coefficients = []
    far = jnp.where(core == 0, 3, 1)
    for text_block, offset in ((text_low, 0), (two_back, 2), (crossed, far), (swapped, 4 - far)):
        owner = (loop_index - offset) % groups
        first_col = (owner * splits + model_index) * rows
        image_part, coefficient = pair_terms(image_low, text_block, positives, first_col)
        image_total = image_total + image_part
        coefficients.append(coefficient)
    image_grad = backward_norm(image_unit, image_inv + zero_of(early), image_total).astype(bf16)

    left, right = image_grad[:, :half], image_grad[:, half:]
    first = z_lo == 0
    mine = jnp.where(first, left, right)
    theirs = moved(jnp.where(first, right, left), other_z_lo)
    both = jnp.where(first, jnp.stack([mine, theirs]), jnp.stack([theirs, mine]))
    gathered = lax.all_gather(
        both.reshape(Z_LO * rows, half),
        "mp",
        axis=0,
        tiled=True,
        axis_index_groups=[list(range(Y)), list(range(Y, Z_LO * Y))],
    )

    scale = SCALE_T + zero_of(theirs)
    text_parts = [text_terms(image_low, coefficient, scale) for coefficient in coefficients]
    back = moved(text_parts[3].astype(bf16), other_core)
    back_two = moved((text_parts[1] + back.astype(jnp.float32)).astype(bf16), next_chip(-1))
    back_cross = moved(text_parts[2].astype(bf16), cross(-1))
    text_total = text_parts[0] + back_two.astype(jnp.float32) + back_cross.astype(jnp.float32)
    text_grad = backward_norm(text_unit, text_inv, text_total).astype(bf16)

    total = lax.dot_general(
        hidden_both, gathered, (((0,), (0,)), ((), ())), preferred_element_type=jnp.float32
    )
    total = total * (1.0 + zero_of(back_two, back_cross))
    part = total.shape[0] // CORE
    total = total[:part] + moved(total[part:].astype(bf16), other_core).astype(jnp.float32)
    part = part // X
    pieces = [
        moved(
            total[part * k : part * (k + 1)].astype(bf16),
            lambda z_hi, x, core, z_lo, y, k=k: (z_hi, x + k, core, z_lo, y),
        )
        for k in range(1, X)
    ]
    total = total[:part] + sum(piece.astype(jnp.float32) for piece in pieces)
    part = part // Z_HI
    pieces = [
        moved(
            total[part * k : part * (k + 1)].astype(bf16),
            lambda z_hi, x, core, z_lo, y, k=k: (z_hi + k, x, core, z_lo, y),
        )
        for k in range(1, Z_HI)
    ]
    total = total[:part] + sum(piece.astype(jnp.float32) for piece in pieces)
    total = total / math.sqrt(rows * splits * groups)
    own = total[:share]
    rest = moved(total[share:], other_z_lo)
    weight_share = jnp.where(
        first, jnp.concatenate([own, rest], axis=1), jnp.concatenate([rest, own], axis=1)
    )
    return (text_grad, weight_share)


def solution(mesh):
    in_specs = (
        P(("loop", "mp"), None),
        P(("loop", "mp"), None),
        P("loop", "mp"),
        P(("loop", "mp")),
    )
    out_specs = (P(("loop", "mp"), None), P(("mp", "loop"), None))
    return jax.shard_map(local, mesh=mesh, in_specs=in_specs, out_specs=out_specs, check_vma=False)
```

```python
import math

import jax
import jax.numpy as jnp
from jax import lax
from jax.experimental import pallas as pl
from jax.experimental.pallas import tpu as pltpu
from jax.sharding import PartitionSpec as P

SCALE_T = 10.0
BIAS_T = -1.0
EPSILON = 1e-06

Z_HI, X, CORE, Z_LO, Y = 4, 4, 2, 2, 8


def moved(value, where):
    pairs = []
    for source in range(Z_HI * X * CORE * Z_LO * Y):
        rest, y = divmod(source, Y)
        rest, z_lo = divmod(rest, Z_LO)
        rest, core = divmod(rest, CORE)
        z_hi, x = divmod(rest, X)
        target = where(z_hi, x, core, z_lo, y)
        if target is None:
            continue
        a, b, c, d, e = target
        pairs.append((source, ((((a % Z_HI) * X + b % X) * CORE + c % CORE) * Z_LO + d % Z_LO) * Y + e % Y))
    return lax.ppermute(value, ("loop", "mp"), pairs)


def next_chip(by):
    def where(z_hi, x, core, z_lo, y):
        chip = z_hi * X + x + by
        return chip // X, chip % X, core, z_lo, y

    return where


def cross(z_hi, x, core, z_lo, y):
    if core == 1 and x == X - 1:
        return None
    chip = z_hi * X + x + 2 * core
    return chip // X, chip % X, 1 - core, z_lo, y


def along_x(by):
    return lambda z_hi, x, core, z_lo, y: (z_hi, x + by, core, z_lo, y)


def back_along_x(z_hi, x, core, z_lo, y):
    return z_hi, x - 2 * (1 - core), 1 - core, z_lo, y


def back_z(z_hi, x, core, z_lo, y):
    if x == X - 1 or (x == X - 2 and core == 1):
        return z_hi - 1, x, core, z_lo, y
    return None


def next_y(by):
    return lambda z_hi, x, core, z_lo, y: (z_hi, x, core, z_lo, y + by)


def third_hop(z_hi, x, core, z_lo, y):
    return (z_hi, 1, 0, z_lo, y) if x == 0 and core == 1 else None


def zero_of(value):
    return jnp.minimum(jnp.abs(value[0, 0].astype(jnp.float32)), 0.0)


def zeros_of(value, rows):
    return jnp.minimum(jnp.abs(value[:rows, :1].astype(jnp.float32)), 0.0)


def other_core(z_hi, x, core, z_lo, y):
    return z_hi, x, 1 - core, z_lo, y


def other_z_lo(z_hi, x, core, z_lo, y):
    return z_hi, x, core, 1 - z_lo, y


def normalize(values):
    widened = values.astype(jnp.float32)
    inverse = lax.rsqrt(jnp.sum(widened * widened, axis=1, keepdims=True) + EPSILON)
    return (widened * inverse, inverse)


def backward_norm(unit_rows, inverse, upstream):
    return (upstream - unit_rows * jnp.sum(unit_rows * upstream, axis=1, keepdims=True)) * inverse


def pair_terms(image_low, text_low, positives, first_col):
    scores = (
        SCALE_T
        * lax.dot_general(
            image_low, text_low, (((1,), (1,)), ((), ())), preferred_element_type=jnp.float32
        )
        + BIAS_T
    )
    columns = first_col + lax.broadcasted_iota(jnp.int32, scores.shape, 1)
    target = (positives[:, None] == columns).astype(jnp.float32)
    coefficient = (jax.nn.sigmoid(scores) - target).astype(jnp.bfloat16)
    image_part = SCALE_T * jnp.dot(coefficient, text_low, preferred_element_type=jnp.float32)
    return (image_part, coefficient)


def text_terms(image_low, coefficient, scale):
    return scale * lax.dot_general(
        coefficient, image_low, (((0,), (0,)), ((), ())), preferred_element_type=jnp.float32
    )


def weight_product(low, high, blocks, done):
    units, depth = low.shape
    both_rows, width = blocks[0].shape
    rows = both_rows // Z_LO
    tile = 256
    keep = units // CORE

    def kernel(low_ref, high_ref, *rest):
        kept_ref, sent_ref = rest[-2:]
        right = [
            jnp.concatenate([ref[z * rows : (z + 1) * rows] for ref in rest[:Y]])
            for z in range(Z_LO)
        ]
        for at in range(0, units, keep // 2):
            rows_at = slice(at, at + keep // 2)
            value = jnp.dot(low_ref[rows_at], right[0], preferred_element_type=jnp.float32)
            value += jnp.dot(high_ref[rows_at], right[1], preferred_element_type=jnp.float32)
            if at < keep:
                kept_ref[rows_at] = value
            else:
                sent_ref[at - keep : at - keep // 2] = value.astype(sent_ref.dtype)

    whole = pl.BlockSpec((units, depth), lambda n: (0, 0))
    out = pl.BlockSpec((keep, tile), lambda n: (0, n))
    return pl.pallas_call(
        kernel,
        grid=(width // tile,),
        in_specs=[whole, whole]
        + [pl.BlockSpec((both_rows, tile), lambda n: (0, n))] * len(blocks)
        + [pl.BlockSpec(memory_space=pl.ANY)] * len(done),
        out_specs=[out, out],
        out_shape=[
            jax.ShapeDtypeStruct((keep, width), jnp.float32),
            jax.ShapeDtypeStruct((keep, width), jnp.bfloat16),
        ],
        compiler_params=pltpu.CompilerParams(vmem_limit_bytes=32 * 2**20),
        cost_estimate=pl.CostEstimate(
            flops=4 * units * depth * width, bytes_accessed=12 * 2**20, transcendentals=0
        ),
    )(low, high, *blocks, *done)


def local(img_emb, txt_emb, hidden, positives):
    bf16 = jnp.bfloat16
    loop_index = lax.axis_index("loop")
    model_index = lax.axis_index("mp")
    core = loop_index % CORE
    x = (loop_index // CORE) % X
    z_hi = loop_index // (CORE * X)
    z_lo = model_index // Y
    groups = lax.axis_size("loop")
    splits = lax.axis_size("mp")
    rows, width = img_emb.shape
    half = width // Z_LO
    units = hidden.shape[1]
    share = units // groups

    text_unit, text_inv = normalize(txt_emb)
    text_low = text_unit.astype(bf16)
    image_unit, image_inv = normalize(img_emb)
    image_low = image_unit.astype(bf16)
    two_back = moved(text_low, next_chip(1))
    crossed = moved(text_low, cross)
    swapped = moved(two_back, other_core)
    crossed = jnp.where((x == 1) & (core == 0), moved(two_back, third_hop), crossed)

    place = lax.broadcasted_iota(jnp.int32, (units, Z_LO * units), 1)
    at_core = (place // (Z_LO * units // CORE) + core) % CORE
    at_chip = (place // (Z_LO * share)) % (X * Z_HI)
    unit = (at_chip * CORE + at_core) * share + place % share
    here = lax.broadcasted_iota(jnp.int32, place.shape, 0) == unit
    which = (place // share) % Z_LO
    pick = (here & (which == 0)).astype(bf16), (here & (which == 1)).astype(bf16)

    def both_units(own, before):
        own = jnp.roll(own, -rows * (model_index % Y), axis=0)
        other = moved(own + zero_of(before).astype(bf16), other_z_lo)
        units_first = (((0,), (1,)), ((), ()))
        mixed = lax.dot_general(pick[0], own, units_first, preferred_element_type=bf16)
        mixed += lax.dot_general(pick[1], other, units_first, preferred_element_type=bf16)
        return mixed, other

    image_total = jnp.zeros(img_emb.shape, jnp.float32)
    coefficients = []
    far = jnp.where(core == 0, 3, 1)
    for text_block, offset in ((text_low, 0), (two_back, 2), (crossed, far), (swapped, 4 - far)):
        owner = (loop_index - offset) % groups
        first_col = (owner * splits + model_index) * rows
        image_part, coefficient = pair_terms(image_low, text_block, positives, first_col)
        image_total = image_total + image_part
        coefficients.append(coefficient)
    low, early = both_units(hidden[: Y * rows], coefficients[0])
    image_grad = backward_norm(image_unit, image_inv + zeros_of(early, rows), image_total).astype(bf16)

    left, right = image_grad[:, :half], image_grad[:, half:]
    first = z_lo == 0
    mine = jnp.where(first, left, right)
    theirs = moved(jnp.where(first, right, left), other_z_lo)
    both = jnp.where(first, jnp.stack([mine, theirs]), jnp.stack([theirs, mine]))
    block = both.reshape(Z_LO * rows, half)
    got = [block] + [None] * (Y - 1)
    forward = backward = block
    for step in range(1, Y // 2 + 1):
        forward = got[Y - step] = moved(forward, next_y(1))
        if step < Y // 2:
            backward = got[step] = moved(backward, next_y(-1))

    scale = SCALE_T + zeros_of(image_grad, rows)
    text_parts = [text_terms(image_low, coefficient, scale) for coefficient in coefficients]
    back = moved(text_parts[3].astype(bf16), other_core)
    back_two = moved((text_parts[1] + back.astype(jnp.float32)).astype(bf16), along_x(-1))
    back_cross = moved(text_parts[2].astype(bf16), back_along_x)
    back_two, back_cross = back_two.astype(jnp.float32), back_cross.astype(jnp.float32)
    far_two, far_cross = x == X - 1, (x >= X - 2) & (core == 1)
    leaving = jnp.where(far_two, back_two, 0.0) + jnp.where(far_cross, back_cross, 0.0)
    staying = jnp.where(far_two, 0.0, back_two) + jnp.where(far_cross, 0.0, back_cross)
    back_far = moved(leaving.astype(bf16), back_z)
    text_total = text_parts[0] + staying + back_far.astype(jnp.float32)
    text_grad = backward_norm(text_unit, text_inv, text_total).astype(bf16)

    high, _ = both_units(hidden[Y * rows :], image_grad)
    kept, sent = weight_product(low, high, got, (back_far,))
    total = kept + moved(sent, other_core).astype(jnp.float32)
    part = total.shape[0]
    pieces = lax.all_to_all(
        total.astype(bf16).reshape(X * Z_HI, part // (X * Z_HI), half),
        "loop",
        0,
        0,
        tiled=True,
        axis_index_groups=[list(range(c, groups, CORE)) for c in range(CORE)],
    )
    total = jnp.sum(pieces.astype(jnp.float32), axis=0)
    total = total / math.sqrt(rows * splits * groups)
    own = total[:share]
    rest = moved(total[share:], other_z_lo)
    weight_share = jnp.where(
        first, jnp.concatenate([own, rest], axis=1), jnp.concatenate([rest, own], axis=1)
    )
    return (text_grad, weight_share)


def solution(mesh):
    in_specs = (
        P(("loop", "mp"), None),
        P(("loop", "mp"), None),
        P("loop", "mp"),
        P(("loop", "mp")),
    )
    out_specs = (P(("loop", "mp"), None), P(("mp", "loop"), None))
    return jax.shard_map(local, mesh=mesh, in_specs=in_specs, out_specs=out_specs, check_vma=False)
```

```python
import math

import jax
import jax.numpy as jnp
from jax import lax
from jax.experimental import pallas as pl
from jax.experimental.pallas import tpu as pltpu
from jax.sharding import PartitionSpec as P

SCALE_T = 10.0
BIAS_T = -1.0
EPSILON = 1e-06

Z_HI, X, CORE, Z_LO, Y = 4, 4, 2, 2, 8


def moved(value, where):
    pairs = []
    for source in range(Z_HI * X * CORE * Z_LO * Y):
        rest, y = divmod(source, Y)
        rest, z_lo = divmod(rest, Z_LO)
        rest, core = divmod(rest, CORE)
        z_hi, x = divmod(rest, X)
        target = where(z_hi, x, core, z_lo, y)
        if target is None:
            continue
        a, b, c, d, e = target
        pairs.append((source, ((((a % Z_HI) * X + b % X) * CORE + c % CORE) * Z_LO + d % Z_LO) * Y + e % Y))
    return lax.ppermute(value, ("loop", "mp"), pairs)


def next_chip(by):
    def where(z_hi, x, core, z_lo, y):
        chip = z_hi * X + x + by
        return chip // X, chip % X, core, z_lo, y

    return where


def cross(z_hi, x, core, z_lo, y):
    if core == 1 and x == X - 1:
        return None
    chip = z_hi * X + x + 2 * core
    return chip // X, chip % X, 1 - core, z_lo, y


def along_x(by):
    return lambda z_hi, x, core, z_lo, y: (z_hi, x + by, core, z_lo, y)


def back_along_x(z_hi, x, core, z_lo, y):
    return z_hi, x - 2 * (1 - core), 1 - core, z_lo, y


def back_z(z_hi, x, core, z_lo, y):
    if x == X - 1 or (x == X - 2 and core == 1):
        return z_hi - 1, x, core, z_lo, y
    return None


def next_y(by):
    return lambda z_hi, x, core, z_lo, y: (z_hi, x, core, z_lo, y + by)


def third_hop(z_hi, x, core, z_lo, y):
    return (z_hi, 1, 0, z_lo, y) if x == 0 and core == 1 else None


def zero_of(value):
    return jnp.minimum(jnp.abs(value[0, 0].astype(jnp.float32)), 0.0)


def zeros_of(value, rows):
    return jnp.minimum(jnp.abs(value[:rows, :1].astype(jnp.float32)), 0.0)


def other_core(z_hi, x, core, z_lo, y):
    return z_hi, x, 1 - core, z_lo, y


def other_z_lo(z_hi, x, core, z_lo, y):
    return z_hi, x, core, 1 - z_lo, y


def normalize(values):
    widened = values.astype(jnp.float32)
    inverse = lax.rsqrt(jnp.sum(widened * widened, axis=1, keepdims=True) + EPSILON)
    return (widened * inverse, inverse)


def backward_norm(unit_rows, inverse, upstream):
    return (upstream - unit_rows * jnp.sum(unit_rows * upstream, axis=1, keepdims=True)) * inverse


def pair_terms(image_low, text_low, positives, first_col):
    scores = (
        SCALE_T
        * lax.dot_general(
            image_low, text_low, (((1,), (1,)), ((), ())), preferred_element_type=jnp.float32
        )
        + BIAS_T
    )
    columns = first_col + lax.broadcasted_iota(jnp.int32, scores.shape, 1)
    target = (positives[:, None] == columns).astype(jnp.float32)
    coefficient = (jax.nn.sigmoid(scores) - target).astype(jnp.bfloat16)
    image_part = SCALE_T * jnp.dot(coefficient, text_low, preferred_element_type=jnp.float32)
    return (image_part, coefficient)


def text_terms(image_low, coefficient, scale):
    return scale * lax.dot_general(
        coefficient, image_low, (((0,), (0,)), ((), ())), preferred_element_type=jnp.float32
    )


def weight_product(hidden_units, blocks, done):
    units, depth = hidden_units.shape
    rows, width = blocks[0].shape
    tile = 256
    steps = width // (2 * tile)
    keep = 2 * units // CORE
    share = units // (CORE * X * Z_HI * Z_LO)

    def kernel(hidden_ref, *rest):
        kept_ref, sent_ref, laid = rest[-3:]
        left = jnp.concatenate([ref[...] for ref in rest[:Y]])
        right = jnp.concatenate([ref[...] for ref in rest[Y : 2 * Y]])
        step = units // CORE
        for at in range(0, units, step):
            lines = hidden_ref[at : at + step]
            to = kept_ref if at == 0 else laid
            for side, columns in enumerate((left, right)):
                value = jnp.dot(lines, columns, preferred_element_type=jnp.float32)
                for k in range(step // share):
                    first = (2 * k + side) * share
                    to[first : first + share] = value[k * share : (k + 1) * share]
        sent_ref[...] = laid[...].astype(sent_ref.dtype)

    out = pl.BlockSpec((keep, tile), lambda n: (0, n))
    return pl.pallas_call(
        kernel,
        grid=(steps,),
        in_specs=[pl.BlockSpec((units, depth), lambda n: (0, 0))]
        + [pl.BlockSpec((rows, tile), lambda n: (0, n))] * Y
        + [pl.BlockSpec((rows, tile), lambda n: (0, n + steps))] * Y
        + [pl.BlockSpec(memory_space=pl.ANY)] * len(done),
        out_specs=[out, out],
        out_shape=[
            jax.ShapeDtypeStruct((keep, width // 2), jnp.float32),
            jax.ShapeDtypeStruct((keep, width // 2), jnp.bfloat16),
        ],
        scratch_shapes=[pltpu.VMEM((keep, tile), jnp.float32)],
        compiler_params=pltpu.CompilerParams(vmem_limit_bytes=40 * 2**20),
        cost_estimate=pl.CostEstimate(
            flops=2 * units * depth * width, bytes_accessed=12 * 2**20, transcendentals=0
        ),
    )(hidden_units, *blocks, *blocks, *done)


def local(img_emb, txt_emb, hidden, positives):
    bf16 = jnp.bfloat16
    loop_index = lax.axis_index("loop")
    model_index = lax.axis_index("mp")
    core = loop_index % CORE
    x = (loop_index // CORE) % X
    z_hi = loop_index // (CORE * X)
    z_lo = model_index // Y
    groups = lax.axis_size("loop")
    splits = lax.axis_size("mp")
    rows, width = img_emb.shape
    units = hidden.shape[1]
    share = units // groups

    text_unit, text_inv = normalize(txt_emb)
    text_low = text_unit.astype(bf16)
    image_unit, image_inv = normalize(img_emb)
    image_low = image_unit.astype(bf16)
    two_back = moved(text_low, next_chip(1))
    crossed = moved(text_low, cross)
    swapped = moved(two_back, other_core)
    crossed = jnp.where((x == 1) & (core == 0), moved(two_back, third_hop), crossed)

    place = lax.broadcasted_iota(jnp.int32, (units, Z_LO * units), 1)
    at_core = (place // (Z_LO * units // CORE) + core) % CORE
    at_chip = (place // (Z_LO * share)) % (X * Z_HI)
    at_z_lo = (place // share) % Z_LO
    unit = (at_chip * CORE + at_core) * share + place % share
    here = lax.broadcasted_iota(jnp.int32, place.shape, 0) == unit
    pick = (here & (at_z_lo == z_lo)).astype(bf16), (here & (at_z_lo != z_lo)).astype(bf16)
    column_index = lax.broadcasted_iota(jnp.int32, (rows, rows), 1)

    def in_ring_order(low):
        at = jnp.where(low, 0, Y * rows)
        return jnp.roll(lax.dynamic_slice_in_dim(hidden, at, Y * rows), -rows * (model_index % Y), 0)

    first = z_lo == 0

    def all_units(before):
        units_first = (((0,), (1,)), ((), ()))
        own = in_ring_order(first) + zero_of(before).astype(bf16)
        mixed = lax.dot_general(pick[0], own, units_first, preferred_element_type=bf16)
        other = moved(in_ring_order(~first) + zero_of(mixed).astype(bf16), other_z_lo)
        mixed += lax.dot_general(pick[1], other, units_first, preferred_element_type=bf16)
        return mixed, other

    image_total = jnp.zeros(img_emb.shape, jnp.float32)
    coefficients = []
    far = jnp.where(core == 0, 3, 1)
    for text_block, offset in ((text_low, 0), (two_back, 2), (crossed, far), (swapped, 4 - far)):
        owner = (loop_index - offset) % groups
        first_col = (owner * splits + model_index) * rows
        image_part, coefficient = pair_terms(image_low, text_block, positives, first_col)
        image_total = image_total + image_part
        coefficients.append(coefficient)
    hidden_units, early = all_units(coefficients[0])
    image_grad = backward_norm(image_unit, image_inv, image_total).astype(bf16)

    block = image_grad
    got = [block] + [None] * (Y - 1)
    forward = backward = block
    for step in range(1, Y // 2 + 1):
        forward = got[Y - step] = moved(forward, next_y(1))
        if step < Y // 2:
            backward = got[step] = moved(backward, next_y(-1))

    scale = SCALE_T + zeros_of(image_grad, rows) + zeros_of(early, rows)
    text_parts = [text_terms(image_low, coefficient, scale) for coefficient in coefficients]
    back = moved(text_parts[3].astype(bf16), other_core)
    back_two = moved((text_parts[1] + back.astype(jnp.float32)).astype(bf16), along_x(-1))
    back_cross = moved(text_parts[2].astype(bf16), back_along_x)
    back_two, back_cross = back_two.astype(jnp.float32), back_cross.astype(jnp.float32)
    far_two, far_cross = x == X - 1, (x >= X - 2) & (core == 1)
    leaving = jnp.where(far_two, back_two, 0.0) + jnp.where(far_cross, back_cross, 0.0)
    staying = jnp.where(far_two, 0.0, back_two) + jnp.where(far_cross, 0.0, back_cross)
    back_far = moved(leaving.astype(bf16), back_z)
    text_total = text_parts[0] + staying + back_far.astype(jnp.float32)
    text_grad = backward_norm(text_unit, text_inv, text_total).astype(bf16)

    kept, sent = weight_product(hidden_units, got, (back_far,))
    total = kept + moved(sent, other_core).astype(jnp.float32)
    places = X * Z_HI * Z_LO
    peers = [
        [
            (chip * CORE + c) * splits + z * Y + y
            for chip in range(X * Z_HI)
            for z in range(Z_LO)
        ]
        for c in range(CORE)
        for y in range(Y)
    ]
    pieces = lax.all_to_all(
        total.astype(bf16).reshape(places, 2 * share, width // 2),
        ("loop", "mp"),
        0,
        0,
        tiled=True,
        axis_index_groups=peers,
    )
    total = jnp.sum(pieces.astype(jnp.float32), axis=0) / math.sqrt(rows * splits * groups)
    weight_share = jnp.concatenate([total[:share], total[share:]], axis=1)
    return (text_grad, weight_share)


def solution(mesh):
    in_specs = (
        P(("loop", "mp"), None),
        P(("loop", "mp"), None),
        P("loop", "mp"),
        P(("loop", "mp")),
    )
    out_specs = (P(("loop", "mp"), None), P(("mp", "loop"), None))
    return jax.shard_map(local, mesh=mesh, in_specs=in_specs, out_specs=out_specs, check_vma=False)
```

```python
import math

import jax
import jax.numpy as jnp
from jax import lax
from jax.experimental import pallas as pl
from jax.experimental.pallas import tpu as pltpu
from jax.sharding import PartitionSpec as P

SCALE_T = 10.0
BIAS_T = -1.0
EPSILON = 1e-06

Z_HI, X, CORE, Z_LO, Y = 4, 4, 2, 2, 8


def moved(value, where):
    pairs = []
    for source in range(Z_HI * X * CORE * Z_LO * Y):
        rest, y = divmod(source, Y)
        rest, z_lo = divmod(rest, Z_LO)
        rest, core = divmod(rest, CORE)
        z_hi, x = divmod(rest, X)
        target = where(z_hi, x, core, z_lo, y)
        if target is None:
            continue
        a, b, c, d, e = target
        pairs.append((source, ((((a % Z_HI) * X + b % X) * CORE + c % CORE) * Z_LO + d % Z_LO) * Y + e % Y))
    return lax.ppermute(value, ("loop", "mp"), pairs)


def next_chip(by):
    def where(z_hi, x, core, z_lo, y):
        chip = z_hi * X + x + by
        return chip // X, chip % X, core, z_lo, y

    return where


def cross(z_hi, x, core, z_lo, y):
    if core == 1 and x == X - 1:
        return None
    chip = z_hi * X + x + 2 * core
    return chip // X, chip % X, 1 - core, z_lo, y


def along_x(by):
    return lambda z_hi, x, core, z_lo, y: (z_hi, x + by, core, z_lo, y)


def back_along_x(z_hi, x, core, z_lo, y):
    return z_hi, x - 2 * (1 - core), 1 - core, z_lo, y


def back_z(z_hi, x, core, z_lo, y):
    if x == X - 1 or (x == X - 2 and core == 1):
        return z_hi - 1, x, core, z_lo, y
    return None


def next_y(by):
    return lambda z_hi, x, core, z_lo, y: (z_hi, x, core, z_lo, y + by)


def third_hop(z_hi, x, core, z_lo, y):
    return (z_hi, 1, 0, z_lo, y) if x == 0 and core == 1 else None


def zero_of(value):
    return jnp.minimum(jnp.abs(value[0, 0].astype(jnp.float32)), 0.0)


def zeros_of(value, rows):
    return jnp.minimum(jnp.abs(value[:rows, :1].astype(jnp.float32)), 0.0)


def other_core(z_hi, x, core, z_lo, y):
    return z_hi, x, 1 - core, z_lo, y


def other_z_lo(z_hi, x, core, z_lo, y):
    return z_hi, x, core, 1 - z_lo, y


def normalize(values):
    widened = values.astype(jnp.float32)
    inverse = lax.rsqrt(jnp.sum(widened * widened, axis=1, keepdims=True) + EPSILON)
    return (widened * inverse, inverse)


def backward_norm(unit_rows, inverse, upstream):
    return (upstream - unit_rows * jnp.sum(unit_rows * upstream, axis=1, keepdims=True)) * inverse


def pair_terms(image_low, text_low, positives, first_col):
    scores = (
        SCALE_T
        * lax.dot_general(
            image_low, text_low, (((1,), (1,)), ((), ())), preferred_element_type=jnp.float32
        )
        + BIAS_T
    )
    columns = first_col + lax.broadcasted_iota(jnp.int32, scores.shape, 1)
    target = (positives[:, None] == columns).astype(jnp.float32)
    coefficient = (jax.nn.sigmoid(scores) - target).astype(jnp.bfloat16)
    image_part = SCALE_T * jnp.dot(coefficient, text_low, preferred_element_type=jnp.float32)
    return (image_part, coefficient)


def text_terms(image_low, coefficient, scale):
    return scale * lax.dot_general(
        coefficient, image_low, (((0,), (0,)), ((), ())), preferred_element_type=jnp.float32
    )


def weight_product(hidden_units, blocks, done):
    units, depth = hidden_units.shape
    rows, width = blocks[0].shape
    tile = 256
    steps = width // (2 * tile)
    keep = 2 * units // CORE
    share = units // (CORE * X * Z_HI * Z_LO)

    def kernel(hidden_ref, *rest):
        kept_ref, sent_ref, laid = rest[-3:]
        left = jnp.concatenate([ref[...] for ref in rest[:Y]])
        right = jnp.concatenate([ref[...] for ref in rest[Y : 2 * Y]])
        step = units // CORE
        for at in range(0, units, step):
            lines = hidden_ref[at : at + step]
            to = kept_ref if at == 0 else laid
            for side, columns in enumerate((left, right)):
                value = jnp.dot(lines, columns, preferred_element_type=jnp.float32)
                for k in range(step // share):
                    first = (2 * k + side) * share
                    to[first : first + share] = value[k * share : (k + 1) * share]
        sent_ref[...] = laid[...].astype(sent_ref.dtype)

    out = pl.BlockSpec((keep, tile), lambda n: (0, n))
    return pl.pallas_call(
        kernel,
        grid=(steps,),
        in_specs=[pl.BlockSpec((units, depth), lambda n: (0, 0))]
        + [pl.BlockSpec((rows, tile), lambda n: (0, n))] * Y
        + [pl.BlockSpec((rows, tile), lambda n: (0, n + steps))] * Y
        + [pl.BlockSpec(memory_space=pl.ANY)] * len(done),
        out_specs=[out, out],
        out_shape=[
            jax.ShapeDtypeStruct((keep, width // 2), jnp.float32),
            jax.ShapeDtypeStruct((keep, width // 2), jnp.bfloat16),
        ],
        scratch_shapes=[pltpu.VMEM((keep, tile), jnp.float32)],
        compiler_params=pltpu.CompilerParams(vmem_limit_bytes=40 * 2**20),
        cost_estimate=pl.CostEstimate(
            flops=2 * units * depth * width, bytes_accessed=12 * 2**20, transcendentals=0
        ),
    )(hidden_units, *blocks, *blocks, *done)


def local(img_emb, txt_emb, hidden, positives):
    bf16 = jnp.bfloat16
    loop_index = lax.axis_index("loop")
    model_index = lax.axis_index("mp")
    core = loop_index % CORE
    x = (loop_index // CORE) % X
    z_hi = loop_index // (CORE * X)
    z_lo = model_index // Y
    groups = lax.axis_size("loop")
    splits = lax.axis_size("mp")
    rows, width = img_emb.shape
    units = hidden.shape[1]
    share = units // groups

    text_unit, text_inv = normalize(txt_emb)
    text_low = text_unit.astype(bf16)
    image_unit, image_inv = normalize(img_emb)
    image_low = image_unit.astype(bf16)
    two_back = moved(text_low, next_chip(1))
    crossed = moved(text_low, cross)
    swapped = moved(two_back, other_core)
    crossed = jnp.where((x == 1) & (core == 0), moved(two_back, third_hop), crossed)

    place = lax.broadcasted_iota(jnp.int32, (units, Z_LO * units), 1)
    at_core = (place // (Z_LO * units // CORE) + core) % CORE
    at_chip = (place // (Z_LO * share)) % (X * Z_HI)
    at_z_lo = (place // share) % Z_LO
    unit = (at_chip * CORE + at_core) * share + place % share
    here = lax.broadcasted_iota(jnp.int32, place.shape, 0) == unit
    pick = (here & (at_z_lo == z_lo)).astype(bf16), (here & (at_z_lo != z_lo)).astype(bf16)
    column_index = lax.broadcasted_iota(jnp.int32, (rows, rows), 1)

    def in_ring_order(low):
        at = jnp.where(low, 0, Y * rows)
        return jnp.roll(lax.dynamic_slice_in_dim(hidden, at, Y * rows), -rows * (model_index % Y), 0)

    first = z_lo == 0

    def all_units(before):
        units_first = (((0,), (1,)), ((), ()))
        ordered = zero_of(before).astype(bf16)
        other = moved(in_ring_order(~first) + ordered, other_z_lo)
        own = lax.dot_general(
            pick[0], in_ring_order(first) + ordered, units_first, preferred_element_type=bf16
        )
        return own, other, own + lax.dot_general(
            pick[1], other, units_first, preferred_element_type=bf16
        )

    image_total = jnp.zeros(img_emb.shape, jnp.float32)
    coefficients = []
    far = jnp.where(core == 0, 3, 1)
    for text_block, offset in ((text_low, 0), (two_back, 2), (crossed, far), (swapped, 4 - far)):
        owner = (loop_index - offset) % groups
        first_col = (owner * splits + model_index) * rows
        image_part, coefficient = pair_terms(image_low, text_block, positives, first_col)
        image_total = image_total + image_part
        coefficients.append(coefficient)
    own_units, early, hidden_units = all_units(coefficients[0])
    image_grad = backward_norm(
        image_unit, image_inv + zeros_of(own_units, rows), image_total
    ).astype(bf16)

    block = image_grad
    got = [block] + [None] * (Y - 1)
    forward = backward = block
    for step in range(1, Y // 2 + 1):
        forward = got[Y - step] = moved(forward, next_y(1))
        if step < Y // 2:
            backward = got[step] = moved(backward, next_y(-1))

    scale = SCALE_T + zeros_of(image_grad, rows) + zeros_of(early, rows)
    text_parts = [text_terms(image_low, coefficient, scale) for coefficient in coefficients]
    back = moved(text_parts[3].astype(bf16), other_core)
    back_two = moved((text_parts[1] + back.astype(jnp.float32)).astype(bf16), along_x(-1))
    back_cross = moved(text_parts[2].astype(bf16), back_along_x)
    back_two, back_cross = back_two.astype(jnp.float32), back_cross.astype(jnp.float32)
    far_two, far_cross = x == X - 1, (x >= X - 2) & (core == 1)
    leaving = jnp.where(far_two, back_two, 0.0) + jnp.where(far_cross, back_cross, 0.0)
    staying = jnp.where(far_two, 0.0, back_two) + jnp.where(far_cross, 0.0, back_cross)
    back_far = moved(leaving.astype(bf16), back_z)
    text_total = text_parts[0] + staying + back_far.astype(jnp.float32)
    text_grad = backward_norm(text_unit, text_inv, text_total).astype(bf16)

    kept, sent = weight_product(hidden_units, got, (back_far,))
    total = kept + moved(sent, other_core).astype(jnp.float32)
    places = X * Z_HI * Z_LO
    peers = [
        [
            (chip * CORE + c) * splits + z * Y + y
            for chip in range(X * Z_HI)
            for z in range(Z_LO)
        ]
        for c in range(CORE)
        for y in range(Y)
    ]
    pieces = lax.all_to_all(
        total.astype(bf16).reshape(places, 2 * share, width // 2),
        ("loop", "mp"),
        0,
        0,
        tiled=True,
        axis_index_groups=peers,
    )
    total = jnp.sum(pieces.astype(jnp.float32), axis=0) / math.sqrt(rows * splits * groups)
    weight_share = jnp.concatenate([total[:share], total[share:]], axis=1)
    return (text_grad, weight_share)


def solution(mesh):
    in_specs = (
        P(("loop", "mp"), None),
        P(("loop", "mp"), None),
        P("loop", "mp"),
        P(("loop", "mp")),
    )
    out_specs = (P(("loop", "mp"), None), P(("mp", "loop"), None))
    return jax.shard_map(local, mesh=mesh, in_specs=in_specs, out_specs=out_specs, check_vma=False)
```

```python
import math

import jax
import jax.numpy as jnp
from jax import lax
from jax.experimental import pallas as pl
from jax.experimental.pallas import tpu as pltpu
from jax.sharding import PartitionSpec as P

SCALE_T = 10.0
BIAS_T = -1.0
EPSILON = 1e-06

Z_HI, X, CORE, Z_LO, Y = 4, 4, 2, 2, 8


def moved(value, where):
    pairs = []
    for source in range(Z_HI * X * CORE * Z_LO * Y):
        rest, y = divmod(source, Y)
        rest, z_lo = divmod(rest, Z_LO)
        rest, core = divmod(rest, CORE)
        z_hi, x = divmod(rest, X)
        target = where(z_hi, x, core, z_lo, y)
        if target is None:
            continue
        a, b, c, d, e = target
        pairs.append((source, ((((a % Z_HI) * X + b % X) * CORE + c % CORE) * Z_LO + d % Z_LO) * Y + e % Y))
    return lax.ppermute(value, ("loop", "mp"), pairs)


def next_chip(by):
    def where(z_hi, x, core, z_lo, y):
        chip = z_hi * X + x + by
        return chip // X, chip % X, core, z_lo, y

    return where


def cross(z_hi, x, core, z_lo, y):
    if core == 1 and x == X - 1:
        return None
    chip = z_hi * X + x + 2 * core
    return chip // X, chip % X, 1 - core, z_lo, y


def along_x(by):
    return lambda z_hi, x, core, z_lo, y: (z_hi, x + by, core, z_lo, y)


def back_along_x(z_hi, x, core, z_lo, y):
    return z_hi, x - 2 * (1 - core), 1 - core, z_lo, y


def back_z(z_hi, x, core, z_lo, y):
    if x == X - 1 or (x == X - 2 and core == 1):
        return z_hi - 1, x, core, z_lo, y
    return None


def next_y(by):
    return lambda z_hi, x, core, z_lo, y: (z_hi, x, core, z_lo, y + by)


def third_hop(z_hi, x, core, z_lo, y):
    return (z_hi, 1, 0, z_lo, y) if x == 0 and core == 1 else None


def zero_of(value):
    return jnp.minimum(jnp.abs(value[0, 0].astype(jnp.float32)), 0.0)


def zeros_of(value, rows):
    return jnp.minimum(jnp.abs(value[:rows, :1].astype(jnp.float32)), 0.0)


def other_core(z_hi, x, core, z_lo, y):
    return z_hi, x, 1 - core, z_lo, y


def other_z_lo(z_hi, x, core, z_lo, y):
    return z_hi, x, core, 1 - z_lo, y


def normalize(values):
    widened = values.astype(jnp.float32)
    inverse = lax.rsqrt(jnp.sum(widened * widened, axis=1, keepdims=True) + EPSILON)
    return (widened * inverse, inverse)


def backward_norm(unit_rows, inverse, upstream):
    return (upstream - unit_rows * jnp.sum(unit_rows * upstream, axis=1, keepdims=True)) * inverse


def pair_terms(image_low, text_low, positives, first_col):
    scores = (
        SCALE_T
        * lax.dot_general(
            image_low, text_low, (((1,), (1,)), ((), ())), preferred_element_type=jnp.float32
        )
        + BIAS_T
    )
    columns = first_col + lax.broadcasted_iota(jnp.int32, scores.shape, 1)
    target = (positives[:, None] == columns).astype(jnp.float32)
    coefficient = (jax.nn.sigmoid(scores) - target).astype(jnp.bfloat16)
    image_part = SCALE_T * jnp.dot(coefficient, text_low, preferred_element_type=jnp.float32)
    return (image_part, coefficient)


def text_terms(image_low, coefficient, scale):
    return scale * lax.dot_general(
        coefficient, image_low, (((0,), (0,)), ((), ())), preferred_element_type=jnp.float32
    )


def weight_product(hidden_units, blocks, after, leaving=False):
    units, depth = hidden_units.shape
    rows, width = blocks[0].shape
    tile = 256
    steps = width // (2 * tile)
    share = units // (X * Z_HI * Z_LO)
    count = len(blocks)
    dtype = jnp.bfloat16 if leaving else jnp.float32

    def kernel(*refs):
        left, right = refs[1 : 1 + count], refs[1 + count : 1 + 2 * count]
        out_ref, laid = refs[-2:]
        lines = refs[0][...]
        for side, columns in enumerate((left, right)):
            value = jnp.dot(
                lines,
                jnp.concatenate([ref[...] for ref in columns]),
                preferred_element_type=jnp.float32,
            )
            for k in range(units // share):
                first = (2 * k + side) * share
                laid[first : first + share] = value[k * share : (k + 1) * share]
        out_ref[...] = laid[...].astype(dtype)

    tiles = pl.BlockSpec((2 * units, tile), lambda n: (0, n))
    return pl.pallas_call(
        kernel,
        grid=(steps,),
        in_specs=[pl.BlockSpec((units, depth), lambda n: (0, 0))]
        + [pl.BlockSpec((rows, tile), lambda n: (0, n))] * count
        + [pl.BlockSpec((rows, tile), lambda n: (0, n + steps))] * count
        + [pl.BlockSpec(memory_space=pl.ANY)] * len(after),
        out_specs=tiles,
        out_shape=jax.ShapeDtypeStruct((2 * units, width // 2), dtype),
        scratch_shapes=[pltpu.VMEM((2 * units, tile), jnp.float32)],
        compiler_params=pltpu.CompilerParams(vmem_limit_bytes=40 * 2**20),
        cost_estimate=pl.CostEstimate(
            flops=2 * units * rows * count * width, bytes_accessed=6 * 2**20, transcendentals=0
        ),
    )(hidden_units, *blocks, *blocks, *after)


def local(img_emb, txt_emb, hidden, positives):
    bf16 = jnp.bfloat16
    loop_index = lax.axis_index("loop")
    model_index = lax.axis_index("mp")
    core = loop_index % CORE
    x = (loop_index // CORE) % X
    z_hi = loop_index // (CORE * X)
    z_lo = model_index // Y
    groups = lax.axis_size("loop")
    splits = lax.axis_size("mp")
    rows, width = img_emb.shape
    units = hidden.shape[1]
    share = units // groups

    text_unit, text_inv = normalize(txt_emb)
    text_low = text_unit.astype(bf16)
    image_unit, image_inv = normalize(img_emb)
    image_low = image_unit.astype(bf16)
    two_back = moved(text_low, next_chip(1))
    crossed = moved(text_low, cross)
    swapped = moved(two_back, other_core)
    crossed = jnp.where((x == 1) & (core == 0), moved(two_back, third_hop), crossed)

    place = lax.broadcasted_iota(jnp.int32, (units, Z_LO * units), 1)
    at_core = (place // (Z_LO * units // CORE) + core) % CORE
    at_chip = (place // (Z_LO * share)) % (X * Z_HI)
    at_z_lo = (place // share) % Z_LO
    unit = (at_chip * CORE + at_core) * share + place % share
    here = lax.broadcasted_iota(jnp.int32, place.shape, 0) == unit
    pick = (here & (at_z_lo == z_lo)).astype(bf16), (here & (at_z_lo != z_lo)).astype(bf16)
    column_index = lax.broadcasted_iota(jnp.int32, (rows, rows), 1)

    def in_ring_order(low):
        at = jnp.where(low, 0, Y * rows)
        return jnp.roll(lax.dynamic_slice_in_dim(hidden, at, Y * rows), -rows * (model_index % Y), 0)

    first = z_lo == 0

    def all_units(before):
        units_first = (((0,), (1,)), ((), ()))
        ordered = zero_of(before).astype(bf16)
        other = moved(in_ring_order(~first) + ordered, other_z_lo)
        own = lax.dot_general(
            pick[0], in_ring_order(first) + ordered, units_first, preferred_element_type=bf16
        )
        return own, other, own + lax.dot_general(
            pick[1], other, units_first, preferred_element_type=bf16
        )

    image_total = jnp.zeros(img_emb.shape, jnp.float32)
    coefficients = []
    far = jnp.where(core == 0, 3, 1)
    for text_block, offset in ((text_low, 0), (two_back, 2), (crossed, far), (swapped, 4 - far)):
        owner = (loop_index - offset) % groups
        first_col = (owner * splits + model_index) * rows
        image_part, coefficient = pair_terms(image_low, text_block, positives, first_col)
        image_total = image_total + image_part
        coefficients.append(coefficient)
    own_units, early, hidden_units = all_units(coefficients[0])
    image_grad = backward_norm(
        image_unit, image_inv + zeros_of(own_units, rows), image_total
    ).astype(bf16)

    block = image_grad
    got = [block] + [None] * (Y - 1)
    forward = backward = block
    for step in range(1, Y // 2 + 1):
        forward = got[Y - step] = moved(forward, next_y(1))
        if step < Y // 2:
            backward = got[step] = moved(backward, next_y(-1))

    scale = SCALE_T + zeros_of(image_grad, rows) + zeros_of(early, rows)
    text_parts = [text_terms(image_low, coefficient, scale) for coefficient in coefficients]
    back = moved(text_parts[3].astype(bf16), other_core)
    back_two = moved((text_parts[1] + back.astype(jnp.float32)).astype(bf16), along_x(-1))
    back_cross = moved(text_parts[2].astype(bf16), back_along_x)
    back_two, back_cross = back_two.astype(jnp.float32), back_cross.astype(jnp.float32)
    far_two, far_cross = x == X - 1, (x >= X - 2) & (core == 1)
    leaving = jnp.where(far_two, back_two, 0.0) + jnp.where(far_cross, back_cross, 0.0)
    staying = jnp.where(far_two, 0.0, back_two) + jnp.where(far_cross, 0.0, back_cross)
    back_far = moved(leaving.astype(bf16), back_z)
    text_total = text_parts[0] + staying + back_far.astype(jnp.float32)
    text_grad = backward_norm(text_unit, text_inv, text_total).astype(bf16)

    mine, theirs = jnp.split(hidden_units, CORE)
    sent = weight_product(theirs, got, (back_far,), True)
    kept = weight_product(mine, got, ())
    total = kept + moved(sent, other_core).astype(jnp.float32)
    places = X * Z_HI * Z_LO
    peers = [
        [
            (chip * CORE + c) * splits + z * Y + y
            for chip in range(X * Z_HI)
            for z in range(Z_LO)
        ]
        for c in range(CORE)
        for y in range(Y)
    ]
    pieces = lax.all_to_all(
        total.astype(bf16).reshape(places, 2 * share, width // 2),
        ("loop", "mp"),
        0,
        0,
        tiled=True,
        axis_index_groups=peers,
    )
    total = jnp.sum(pieces.astype(jnp.float32), axis=0) / math.sqrt(rows * splits * groups)
    weight_share = jnp.concatenate([total[:share], total[share:]], axis=1)
    return (text_grad, weight_share)


def solution(mesh):
    in_specs = (
        P(("loop", "mp"), None),
        P(("loop", "mp"), None),
        P("loop", "mp"),
        P(("loop", "mp")),
    )
    out_specs = (P(("loop", "mp"), None), P(("mp", "loop"), None))
    return jax.shard_map(local, mesh=mesh, in_specs=in_specs, out_specs=out_specs, check_vma=False)
```
